32 devices in a mesh: dom: 8 (over y, x, core), lat: 4 (over z).
Axes of the slice: x: 2, y: 2, z: 4, core: 2. Of those that a mesh axis runs over, the one named last changes fastest.
Arguments:
- states: float32 [3, 16, 64, 1024], P(None, 'dom', 'lat'), may hold values from -3 to 3
- stir_noise: float32 [2, 16, 64, 1024], P(None, 'dom', 'lat'), may hold values from -1.2 to 1.2
- ancestors: int32 [2, 8, 2], replicated, may hold values from 0 to 3, as said below
Outputs:
- filtered: float32 [3, 16, 64, 1024], P(None, 'dom', 'lat')
The draws below stay inside these ranges and needn't reach their ends.
Inputs may be any that keep to these rules, and one draw needn't show every extreme that they name: An entry from 2 upward names a particle of the preceding island on the loop; in every row ancestors[c, i, :] exactly one entry is 2 or more.
All inputs are finite; a program needn't handle non-finite values.
Results may differ from the reference program's by a relative error of at most 0.0003.
Values sent between devices are 32-bit elements; how exact they have to be, the bound alone decides.
No kernel may reach another device: no remote copies, remote signals or barrier semaphores. Data moves between devices by JAX's collectives and lax.ppermute only.
A program may use at most 64 MiB of HBM per device.

```python
import jax
import jax.numpy as jnp
from jax import lax

P_ISL = 2
NX = 1024
STEPS = 2
FILTER_ROUNDS = 2
ISLANDS = 8
PARTICLES = 16
NY = 64


def draw_ancestors(key, part):
    key_order = jax.random.fold_in(key, 11)
    key_source = jax.random.fold_in(key, 23)
    shape = (FILTER_ROUNDS, ISLANDS, P_ISL)
    scores = jax.random.randint(key_order, shape, 0, 1 << 20) * P_ISL + jnp.arange(P_ISL, dtype=jnp.int32)
    ranking = jnp.argsort(jnp.argsort(scores, axis=-1, stable=True), axis=-1, stable=True)
    foreign = ranking < P_ISL // 2
    donor_particle = jax.random.randint(key_source, shape, 0, P_ISL)
    first_island = (jnp.arange(ISLANDS, dtype=jnp.int32) == 0)[None, :, None]
    donor_particle = jnp.where(first_island, jnp.where(foreign, P_ISL - 1, 0), donor_particle)
    return jnp.where(foreign, P_ISL + donor_particle, donor_particle).astype(jnp.int32)


def levels(key, shape, split, least, top_value):
    def one(dim, parts):
        heights = jax.random.uniform(jax.random.fold_in(jax.random.fold_in(key, 6), dim), (parts,), jnp.float32, least / len(split), top_value / len(split))
        return jnp.repeat(jnp.exp(heights), shape[dim] // parts).reshape((-1,) + (1,) * (len(shape) - dim - 1))

    factor_of = one(*split[0])
    for cut in split[1:]:
        factor_of = factor_of * one(*cut)
    return factor_of


def scatter_about(rng, extent, scale, limit, cuts=(), kind=jnp.bfloat16):
    array = scale * jax.random.normal(rng, extent, jnp.float32)
    if cuts:
        array = array * levels(rng, extent, cuts, -0.22, 0.18)
    return jnp.clip(array, -limit, limit).astype(kind)


def setup_inputs(seed: int = 0) -> dict:
    key_list = jax.random.split(jax.random.key(seed), 4)
    return {
        "states": scatter_about(key_list[0], (3, PARTICLES, NY, NX), 0.5, 3.0, ((1, 8), (2, 4)), jnp.float32),
        "stir_noise": scatter_about(key_list[1], (FILTER_ROUNDS, PARTICLES, NY, NX), 0.2, 1.2, ((1, 8), (2, 4)), jnp.float32),
        "ancestors": draw_ancestors(jax.random.fold_in(key_list[3], 71), 0),
    }


time_step = 0.2
viscosity = 0.05
rotation = 0.3


def eastward(field_amount):
    return jnp.roll(field_amount, -1, axis=-1)


def westward(field_amount):
    return jnp.roll(field_amount, 1, axis=-1)


def slope_x(field_amount):
    return (eastward(field_amount) - westward(field_amount)) * 0.5


def slope_y(field_amount):
    return (field_amount[..., 2:, :] - field_amount[..., :-2, :]) * 0.5


def laplace(field_amount, middle):
    return eastward(middle) + westward(middle) + field_amount[..., 2:, :] + field_amount[..., :-2, :] - 4.0 * middle


def tendency(padded, coriolis):
    height = padded[0]
    zonal = padded[1]
    northward = padded[2]
    height_mid = height[..., 1:-1, :]
    zonal_mid = zonal[..., 1:-1, :]
    north_mid = northward[..., 1:-1, :]
    column_depth = 1.0 + height
    flux_east = column_depth[..., 1:-1, :] * zonal_mid
    flux_north = column_depth * northward
    tend_height = -slope_x(flux_east) - slope_y(flux_north) + viscosity * laplace(height, height_mid)
    tend_zonal = (-zonal_mid * slope_x(zonal_mid) - north_mid * slope_y(zonal) + coriolis * north_mid
                  - slope_x(height_mid) + viscosity * laplace(zonal, zonal_mid))
    tend_north = (-zonal_mid * slope_x(north_mid) - north_mid * slope_y(northward) - coriolis * zonal_mid
                  - slope_y(height) + viscosity * laplace(northward, north_mid))
    return jnp.stack([tend_height, tend_zonal, tend_north])


def coriolis_rows(start_row, row_count, all_rows):
    row_index = start_row + jnp.arange(row_count, dtype=jnp.int32)
    return (rotation * (2.0 * (row_index.astype(jnp.float32) + 0.5) / all_rows - 1.0))[:, None]


def pad_rows(fields):
    return jnp.pad(fields, ((0, 0), (0, 0), (1, 1), (0, 0)))


def heun_step(fields, coriolis):
    first_section = fields + time_step * tendency(pad_rows(fields), coriolis)
    return 0.5 * (fields + first_section + time_step * tendency(pad_rows(first_section), coriolis))


def reference(states, stir_noise, ancestors):
    islands = ancestors.shape[1]
    per_island = ancestors.shape[2]
    total_rows = states.shape[2]
    coriolis = coriolis_rows(0, total_rows, total_rows)
    island_groups = states.reshape(3, islands, per_island, total_rows, -1).transpose(1, 0, 2, 3, 4)
    for cycle_idx in range(FILTER_ROUNDS):
        driving_term = stir_noise[cycle_idx].reshape(islands, per_island, total_rows, -1)

        def predicted_state(paired_inputs):
            island_state, island_noise = paired_inputs
            for step_idx in range(STEPS):
                island_state = heun_step(island_state, coriolis)
            return jnp.concatenate([island_state[0:1] + island_noise[None], island_state[1:]], axis=0)

        island_groups = lax.map(predicted_state, (island_groups, driving_term))
        cycle_parents = ancestors[cycle_idx]

        def resample(island):
            own_state = island_groups[island]
            before = island_groups[(island - 1) % islands]
            pooled = jnp.concatenate([own_state, before], axis=1)
            return jnp.take(pooled, cycle_parents[island], axis=1)

        island_groups = lax.map(resample, jnp.arange(islands, dtype=jnp.int32))
    return island_groups.transpose(1, 0, 2, 3, 4).reshape(states.shape)
```

```python
import functools

import jax
import jax.numpy as jnp
from jax import lax
from jax.experimental import pallas as pl
from jax.experimental.pallas import tpu as pltpu
from jax.sharding import PartitionSpec as P

STEPS = 2
FILTER_ROUNDS = 2

time_step = 0.2
viscosity = 0.05
rotation = 0.3

LANES = 128
TILE = 8
NEAR = 2 * STEPS
HALO = NEAR * FILTER_ROUNDS
VMEM_LIMIT = 16 << 20

diffuse = time_step * viscosity
half = 0.5 * time_step
gravity = half * half
keep = 1.0 - 4.0 * diffuse


def row_tiles(value):
    lead, (rows, columns) = value.shape[:-2], value.shape[-2:]
    blocks = columns // LANES
    value = value.reshape(*lead, rows // TILE, TILE, blocks, LANES)
    return jnp.swapaxes(value, -3, -2).reshape(*lead, rows // TILE, blocks * TILE, LANES)


def from_row_tiles(value):
    lead, (tiles, sublanes) = value.shape[:-3], value.shape[-3:-1]
    blocks = sublanes // TILE
    value = jnp.swapaxes(value.reshape(*lead, tiles, blocks, TILE, LANES), -3, -2)
    return value.reshape(*lead, tiles * TILE, blocks * LANES)


def entries(table, cycle, island):
    lane = lax.broadcasted_iota(jnp.int32, table.shape[2:], 0)[None]
    first, second = (
        jnp.sum(jnp.where(lane == island, table[cycle, slot : slot + 1].astype(jnp.float32), 0.0))
        for slot in range(2)
    )
    return (
        jnp.minimum(first, second).astype(jnp.int32),
        jnp.maximum(first, second).astype(jnp.int32),
        (second > first).astype(jnp.int32),
    )


def prepare(state_ref, noise_ref, table_ref, main, xa, xb, ka, kb, kmain, later, *, islands):
    slots, tiles = state_ref.shape[1], state_ref.shape[2]
    rows = tiles * TILE
    blocks = state_ref.shape[3] // TILE
    island = lax.axis_index("dom")
    odd = lax.rem(lax.axis_index("lat"), 2)
    table = table_ref[...]
    _, wanted, _ = entries(table, 0, lax.rem(island + 1, islands))
    kept, _, _ = entries(table, 0, island)
    sent = jnp.clip(wanted - slots, 0, slots - 1)
    kept = jnp.clip(kept, 0, slots - 1)

    def state_row(field, slot, tile, row):
        value = state_ref[field, slot, tile, pl.ds(row, blocks, stride=TILE), :]
        return value if field == 0 else value * half

    def noise_row(cycle, slot, tile, row):
        return noise_ref[cycle, slot, tile, pl.ds(row, blocks, stride=TILE), :]

    for slot, whole in ((sent, main), (kept, kmain)):
        for field in range(3):
            for row in range(rows):
                whole[field * rows + row] = state_row(field, slot, row // TILE, row % TILE)
        for row in range(rows):
            whole[3 * rows + row] = noise_row(0, slot, row // TILE, row % TILE)
    for slot, edge, bottom in ((sent, xa, 1 - odd), (sent, xb, odd), (kept, ka, 1 - odd), (kept, kb, odd)):
        tile = bottom * (tiles - 1)
        for field in range(3):
            for row in range(HALO):
                edge[field * HALO + row] = state_row(field, slot, tile, row)
        for row in range(NEAR):
            edge[3 * HALO + row] = noise_row(0, slot, tile, bottom * (TILE - NEAR) + row)
    for slot in range(slots):
        for row in range(rows):
            later[slot * rows + row] = noise_row(1, slot, row // TILE, row % TILE)


def tendency_rows(load, store, first, last, coriolis):
    blocks = load(0, first).shape[0]
    lane = lax.broadcasted_iota(jnp.int32, (blocks, LANES), 1)
    at_end, at_start = lane == LANES - 1, lane == 0

    def east(value):
        turned = pltpu.roll(value, LANES - 1, 1)
        return jnp.where(at_end, pltpu.roll(turned, blocks - 1, 0), turned)

    def west(value):
        turned = pltpu.roll(value, 1, 1)
        return jnp.where(at_start, pltpu.roll(turned, 1, 0), turned)

    def column(row):
        h, u, v = (load(field, row) for field in range(3))
        minus, plus = diffuse - v, diffuse + v
        return h, u, v, minus, plus, h * minus - v, h * plus + v

    below, here = column(first - 1), column(first)
    for row in range(first, last):
        above = column(row + 1)
        h, u, v, v_minus, v_plus, _, _ = here
        h_east, h_west, u_east, u_west, v_east, v_west = east(h), west(h), east(u), west(u), east(v), west(v)
        u_minus, u_plus = diffuse - u, diffuse + u
        turn = coriolis(row)
        h_new = (
            (keep * h + (h_east * (diffuse - u_east) - u_east))
            + (h_west * (diffuse + u_west) + u_west)
            + (above[5] + below[6])
        )
        u_new = (
            (keep * u + u_east * u_minus)
            + (u_west * u_plus + above[1] * v_minus)
            + (below[1] * v_plus + turn * v)
            - gravity * (h_east - h_west)
        )
        v_new = (
            (keep * v + v_east * u_minus)
            + (v_west * u_plus + above[2] * v_minus)
            + (below[2] * v_plus - turn * u)
            - gravity * (above[0] - below[0])
        )
        store(row, h_new, u_new, v_new)
        below, here = here, above


def forecast(table_ref, main, xa, xb, kmain, ka, kb, later, out, state, middle, noise, *, islands, bands, local):
    rows = main.shape[0] // 4
    wide = rows + 2 * HALO
    island, band = lax.axis_index("dom"), lax.axis_index("lat")
    odd = lax.rem(band, 2)
    table = table_ref[...]
    _, _, foreign = entries(table, 0, island)
    if local:
        slot, _, _ = entries(table, 1, island)
    else:
        _, slot, _ = entries(table, 1, lax.rem(island + 1, islands))
        slot = slot - 2
    slot = jnp.clip(slot, 0, 1)
    arrived = slot == foreign
    inside_low = (band > 0).astype(jnp.float32)
    inside_high = (band < bands - 1).astype(jnp.float32)

    def gather(whole, first, second):
        for field in range(3):
            for row in range(rows):
                state[field * wide + HALO + row] = whole[field * rows + row]
        for row in range(rows):
            noise[NEAR + row] = whole[3 * rows + row]
        for edge, high in ((first, 1 - odd), (second, odd)):
            inside = jnp.where(high == 1, inside_high, inside_low)
            start, start_noise = high * (rows + HALO), high * (rows + NEAR)
            for field in range(3):
                for row in range(HALO):
                    state[field * wide + start + row] = edge[field * HALO + row] * inside
            for row in range(NEAR):
                noise[start_noise + row] = edge[3 * HALO + row] * inside

    @pl.when(arrived)
    def _():
        gather(main, xa, xb)

    @pl.when(jnp.logical_not(arrived))
    def _():
        gather(kmain, ka, kb)

    def within(row, value):
        if row < HALO:
            return value * inside_low
        if row >= HALO + rows:
            return value * inside_high
        return value

    start = (band * rows - HALO).astype(jnp.float32)
    slope = time_step * rotation * 2.0 / (rows * bands)
    base = slope * (start + 0.5) - time_step * rotation

    def coriolis(row):
        return base + slope * row

    margin = 0
    for cycle in range(FILTER_ROUNDS):
        for step in range(STEPS):
            last = step == STEPS - 1

            def to_middle(row, *values):
                for field, value in enumerate(values):
                    middle[field * wide + row] = within(row, value)

            def to_state(row, *values, cycle=cycle, last=last):
                final = last and cycle == FILTER_ROUNDS - 1
                for field, value in enumerate(values):
                    value = within(row, 0.5 * (state[field * wide + row] + value))
                    if last and field == 0:
                        if cycle == 0:
                            value = value + noise[row - HALO + NEAR]
                        else:
                            value = value + later[slot * rows + row - HALO]
                    if final:
                        out[field * rows + row - HALO] = value if field == 0 else value * (1.0 / half)
                    else:
                        state[field * wide + row] = value

            margin += 1
            tendency_rows(lambda field, row: state[field * wide + row], to_middle, margin, wide - margin, coriolis)
            margin += 1
            tendency_rows(lambda field, row: middle[field * wide + row], to_state, margin, wide - margin, coriolis)


def finish(table_ref, kept, arrived, out):
    rows = kept.shape[0] // 3
    blocks = out.shape[3] // TILE
    _, _, foreign = entries(table_ref[...], 1, lax.axis_index("dom"))
    for source, slot in ((kept, 1 - foreign), (arrived, foreign)):
        for field in range(3):
            for row in range(rows):
                out[field, slot, row // TILE, pl.ds(row % TILE, blocks, stride=TILE), :] = source[field * rows + row]


def on_chip(kernel, shapes, count, scratch=(), flops=0):
    vmem = pl.BlockSpec(memory_space=pltpu.VMEM)
    return pl.pallas_call(
        kernel,
        out_shape=[jax.ShapeDtypeStruct(shape, jnp.float32) for shape in shapes],
        in_specs=[vmem] * count,
        out_specs=[vmem] * len(shapes),
        scratch_shapes=[pltpu.VMEM(shape, jnp.float32) for shape in scratch],
        cost_estimate=pl.CostEstimate(flops=flops, bytes_accessed=1 << 20, transcendentals=0),
        compiler_params=pltpu.CompilerParams(vmem_limit_bytes=VMEM_LIMIT),
    )


def send(value, place):
    islands, bands = lax.axis_size("dom"), lax.axis_size("lat")
    pairs = []
    for island in range(islands):
        for band in range(bands):
            to_island, to_band = place(island, band)
            pairs.append((island * bands + band, to_island * bands + to_band))
    return lax.ppermute(value, ("dom", "lat"), pairs)


def body(states, stir_noise, ancestors):
    islands, bands = lax.axis_size("dom"), lax.axis_size("lat")
    rows, columns = states.shape[2:]
    blocks = columns // LANES
    wide = rows + 2 * HALO
    state_tiles, noise_tiles = row_tiles(states), row_tiles(stir_noise)
    table = jnp.swapaxes(ancestors, 1, 2)

    def pair(band, turn):
        partner = band + 1 if band % 2 == turn else band - 1
        return partner if 0 <= partner < bands else None

    def following(island, band):
        return (island + 1) % islands, band

    def across(turn, step):
        def place(island, band):
            partner = pair(band, turn)
            if partner is not None:
                return (island + step) % islands, partner
            if step:
                return (island + step) % islands, band
            return (island ^ 1 if islands % 2 == 0 else (island + 1) % islands), band

        return place

    full, edge = (4 * rows, blocks, LANES), (3 * HALO + NEAR, blocks, LANES)
    later_shape = (states.shape[1] * rows, blocks, LANES)
    main, xa, xb, ka, kb, kmain, later = on_chip(
        functools.partial(prepare, islands=islands), [full, edge, edge, edge, edge, full, later_shape], 3
    )(state_tiles, noise_tiles, table)
    main = send(main, following)
    xa, xb = send(xa, across(0, 1)), send(xb, across(1, 1))
    ka, kb = send(ka, across(0, 0)), send(kb, across(1, 0))

    scratch = [(3 * wide, blocks, LANES)] * 2 + [(rows + 2 * NEAR, blocks, LANES)]
    result = (3 * rows, blocks, LANES)
    flops = 60 * wide * columns * 4 * STEPS

    def run(local):
        kernel = functools.partial(forecast, islands=islands, bands=bands, local=local)
        (value,) = on_chip(kernel, [result], 8, scratch, flops)(table, main, xa, xb, kmain, ka, kb, later)
        return value

    arrived = send(run(False), following)
    kept = run(True)
    (out,) = on_chip(finish, [(3,) + state_tiles.shape[1:]], 3)(table, kept, arrived)
    return from_row_tiles(out)


def solution(mesh):
    in_specs = (P(None, "dom", "lat", None), P(None, "dom", "lat", None), P())
    out_specs = P(None, "dom", "lat", None)
    return jax.shard_map(body, mesh=mesh, in_specs=in_specs, out_specs=out_specs, check_vma=False)
```

```python
import functools

import jax
import jax.numpy as jnp
from jax import lax
from jax.experimental import pallas as pl
from jax.experimental.pallas import tpu as pltpu
from jax.sharding import PartitionSpec as P

STEPS = 2
FILTER_ROUNDS = 2

time_step = 0.2
viscosity = 0.05
rotation = 0.3

LANES = 128
TILE = 8
NEAR = 2 * STEPS
HALO = NEAR * FILTER_ROUNDS
VMEM_LIMIT = 16 << 20

diffuse = time_step * viscosity
half = 0.5 * time_step
gravity = half * half
keep = 1.0 - 4.0 * diffuse


def row_tiles(value):
    lead, (rows, columns) = value.shape[:-2], value.shape[-2:]
    blocks = columns // LANES
    value = value.reshape(*lead, rows // TILE, TILE, blocks, LANES)
    return jnp.swapaxes(value, -3, -2).reshape(*lead, rows // TILE, blocks * TILE, LANES)


def from_row_tiles(value):
    lead, (tiles, sublanes) = value.shape[:-3], value.shape[-3:-1]
    blocks = sublanes // TILE
    value = jnp.swapaxes(value.reshape(*lead, tiles, blocks, TILE, LANES), -3, -2)
    return value.reshape(*lead, tiles * TILE, blocks * LANES)


def entries(table, cycle, island):
    lane = lax.broadcasted_iota(jnp.int32, table.shape[2:], 0)[None]
    first, second = (
        jnp.sum(jnp.where(lane == island, table[cycle, slot : slot + 1].astype(jnp.float32), 0.0))
        for slot in range(2)
    )
    return (
        jnp.minimum(first, second).astype(jnp.int32),
        jnp.maximum(first, second).astype(jnp.int32),
        (second > first).astype(jnp.int32),
    )


def collect(state_hbm, noise_hbm, table_hbm, main, state_ref, noise_ref, table_ref, done, *, islands):
    copies = [
        pltpu.make_async_copy(source, target, done.at[index])
        for index, (source, target) in enumerate(
            ((table_hbm, table_ref), (state_hbm, state_ref), (noise_hbm.at[0], noise_ref.at[0]), (noise_hbm.at[1], noise_ref.at[1]))
        )
    ]
    for copy in copies:
        copy.start()
    slots, tiles = state_ref.shape[1], state_ref.shape[2]
    rows = tiles * TILE
    copies[0].wait()
    _, wanted, _ = entries(table_ref[...], 0, lax.rem(lax.axis_index("dom") + 1, islands))
    sent = jnp.clip(wanted - slots, 0, slots - 1)
    copies[1].wait()
    for field in range(3):
        for row in range(rows):
            main[field * rows + row] = state_row(state_ref, field, sent, row // TILE, row % TILE)
    copies[2].wait()
    for row in range(rows):
        main[3 * rows + row] = noise_row(noise_ref, 0, sent, row // TILE, row % TILE)
    copies[3].wait()


def state_row(state_ref, field, slot, tile, row):
    blocks = state_ref.shape[3] // TILE
    value = state_ref[field, slot, tile, pl.ds(row, blocks, stride=TILE), :]
    return value if field == 0 else value * half


def noise_row(noise_ref, cycle, slot, tile, row):
    blocks = noise_ref.shape[3] // TILE
    return noise_ref[cycle, slot, tile, pl.ds(row, blocks, stride=TILE), :]


def edges(state_ref, noise_ref, table_ref, xa, xb, ka, kb, kmain, later, *, islands):
    slots, tiles = state_ref.shape[1], state_ref.shape[2]
    rows = tiles * TILE
    island = lax.axis_index("dom")
    odd = lax.rem(lax.axis_index("lat"), 2)
    table = table_ref[...]
    _, wanted, _ = entries(table, 0, lax.rem(island + 1, islands))
    kept, _, _ = entries(table, 0, island)
    sent = jnp.clip(wanted - slots, 0, slots - 1)
    kept = jnp.clip(kept, 0, slots - 1)
    for slot, edge, bottom in ((sent, xa, 1 - odd), (sent, xb, odd), (kept, ka, 1 - odd), (kept, kb, odd)):
        tile = bottom * (tiles - 1)
        for field in range(3):
            for row in range(HALO):
                edge[field * HALO + row] = state_row(state_ref, field, slot, tile, row)
        for row in range(NEAR):
            edge[3 * HALO + row] = noise_row(noise_ref, 0, slot, tile, bottom * (TILE - NEAR) + row)
    for field in range(3):
        for row in range(rows):
            kmain[field * rows + row] = state_row(state_ref, field, kept, row // TILE, row % TILE)
    for row in range(rows):
        kmain[3 * rows + row] = noise_row(noise_ref, 0, kept, row // TILE, row % TILE)
    for slot in range(slots):
        for row in range(rows):
            later[slot * rows + row] = noise_row(noise_ref, 1, slot, row // TILE, row % TILE)


def tendency_rows(load, store, first, last, coriolis):
    blocks = load(0, first).shape[0]
    lane = lax.broadcasted_iota(jnp.int32, (blocks, LANES), 1)
    at_end, at_start = lane == LANES - 1, lane == 0

    def east(value):
        turned = pltpu.roll(value, LANES - 1, 1)
        return jnp.where(at_end, pltpu.roll(turned, blocks - 1, 0), turned)

    def west(value):
        turned = pltpu.roll(value, 1, 1)
        return jnp.where(at_start, pltpu.roll(turned, 1, 0), turned)

    def column(row):
        h, u, v = (load(field, row) for field in range(3))
        minus, plus = diffuse - v, diffuse + v
        return h, u, v, minus, plus, h * minus - v, h * plus + v

    below, here = column(first - 1), column(first)
    for row in range(first, last):
        above = column(row + 1)
        h, u, v, v_minus, v_plus, _, _ = here
        h_east, h_west, u_east, u_west, v_east, v_west = east(h), west(h), east(u), west(u), east(v), west(v)
        u_minus, u_plus = diffuse - u, diffuse + u
        turn = coriolis(row)
        h_new = (
            (keep * h + (h_east * (diffuse - u_east) - u_east))
            + (h_west * (diffuse + u_west) + u_west)
            + (above[5] + below[6])
        )
        u_new = (
            (keep * u + u_east * u_minus)
            + (u_west * u_plus + above[1] * v_minus)
            + (below[1] * v_plus + turn * v)
            - gravity * (h_east - h_west)
        )
        v_new = (
            (keep * v + v_east * u_minus)
            + (v_west * u_plus + above[2] * v_minus)
            + (below[2] * v_plus - turn * u)
            - gravity * (above[0] - below[0])
        )
        store(row, h_new, u_new, v_new)
        below, here = here, above


def forecast(slot, table, sources, out, state, middle, noise, bands):
    main, xa, xb, kmain, ka, kb, later = sources
    rows = main.shape[0] // 4
    blocks = main.shape[1]
    wide = rows + 2 * HALO
    island, band = lax.axis_index("dom"), lax.axis_index("lat")
    odd = lax.rem(band, 2)
    _, _, foreign = entries(table, 0, island)
    slot = jnp.clip(slot, 0, 1)
    arrived = slot == foreign
    inside_low = (band > 0).astype(jnp.float32)
    inside_high = (band < bands - 1).astype(jnp.float32)

    def gather(whole, first, second):
        for field in range(3):
            for row in range(rows):
                state[field * wide + HALO + row] = whole[field * rows + row]
        for row in range(rows):
            noise[NEAR + row] = whole[3 * rows + row]
        for edge, high in ((first, 1 - odd), (second, odd)):
            inside = jnp.where(high == 1, inside_high, inside_low)
            start, start_noise = high * (rows + HALO), high * (rows + NEAR)
            for field in range(3):
                for row in range(HALO):
                    state[field * wide + start + row] = edge[field * HALO + row] * inside
            for row in range(NEAR):
                noise[start_noise + row] = edge[3 * HALO + row] * inside

    @pl.when(arrived)
    def _():
        gather(main, xa, xb)

    @pl.when(jnp.logical_not(arrived))
    def _():
        gather(kmain, ka, kb)

    def within(row, value):
        if row < HALO:
            return value * inside_low
        if row >= HALO + rows:
            return value * inside_high
        return value

    start = (band * rows - HALO).astype(jnp.float32)
    slope = time_step * rotation * 2.0 / (rows * bands)
    base = slope * (start + 0.5) - time_step * rotation

    def coriolis(row):
        return base + slope * row

    margin = 0
    for cycle in range(FILTER_ROUNDS):
        for step in range(STEPS):
            last = step == STEPS - 1

            def to_middle(row, *values):
                for field, value in enumerate(values):
                    middle[field * wide + row] = within(row, value)

            def to_state(row, *values, cycle=cycle, last=last):
                final = last and cycle == FILTER_ROUNDS - 1
                for field, value in enumerate(values):
                    value = within(row, 0.5 * (state[field * wide + row] + value))
                    if last and field == 0:
                        if cycle == 0:
                            value = value + noise[row - HALO + NEAR]
                        else:
                            value = value + later[slot * rows + row - HALO]
                    if final:
                        own = row - HALO
                        value = value if field == 0 else value * (1.0 / half)
                        out[field, own // TILE, pl.ds(own % TILE, blocks, stride=TILE), :] = value
                    else:
                        state[field * wide + row] = value

            margin += 1
            tendency_rows(lambda field, row: state[field * wide + row], to_middle, margin, wide - margin, coriolis)
            margin += 1
            tendency_rows(lambda field, row: middle[field * wide + row], to_state, margin, wide - margin, coriolis)


def wanted_slot(table, islands):
    _, slot, _ = entries(table, 1, lax.rem(lax.axis_index("dom") + 1, islands))
    return slot - 2


def kept_slot(table):
    slot, _, _ = entries(table, 1, lax.axis_index("dom"))
    return slot


def odd_island():
    return lax.rem(lax.axis_index("dom"), 2)


def payload_odd(table_ref, *refs, islands, bands):
    *sources, out, state, middle, noise = refs

    @pl.when(odd_island() == 1)
    def _():
        table = table_ref[...]
        forecast(wanted_slot(table, islands), table, sources, out, state, middle, noise, bands)


def payload_even(table_ref, *refs, islands, bands):
    *sources, out, state, middle, noise = refs
    table = table_ref[...]
    slot = jnp.where(odd_island() == 1, kept_slot(table), wanted_slot(table, islands))
    forecast(slot, table, sources, out, state, middle, noise, bands)


def keep_local(table_ref, *refs, bands):
    *sources, out, state, middle, noise = refs

    @pl.when(odd_island() == 0)
    def _():
        table = table_ref[...]
        forecast(kept_slot(table), table, sources, out, state, middle, noise, bands)


def finish(table_ref, far, second, near, third, out, done):
    _, _, foreign = entries(table_ref[...], 1, lax.axis_index("dom"))

    def write(kept, taken):
        copies = [
            pltpu.make_async_copy(kept, out.at[:, 1 - foreign], done.at[0]),
            pltpu.make_async_copy(taken, out.at[:, foreign], done.at[1]),
        ]
        for copy in copies:
            copy.start()
        for copy in copies:
            copy.wait()

    @pl.when(odd_island() == 1)
    def _():
        write(second, near)

    @pl.when(odd_island() == 0)
    def _():
        write(third, far)


VMEM = pl.BlockSpec(memory_space=pltpu.VMEM)
HBM = pl.BlockSpec(memory_space=pltpu.HBM)


def on_chip(kernel, ins, outs, scratch=(), flops=0, **more):
    return pl.pallas_call(
        kernel,
        in_specs=ins,
        out_shape=[jax.ShapeDtypeStruct(shape, dtype) for _, shape, dtype in outs],
        out_specs=[spec for spec, _, _ in outs],
        scratch_shapes=scratch,
        cost_estimate=pl.CostEstimate(flops=flops, bytes_accessed=1 << 20, transcendentals=0),
        compiler_params=pltpu.CompilerParams(vmem_limit_bytes=VMEM_LIMIT),
        **more,
    )


def send(value, place):
    islands, bands = lax.axis_size("dom"), lax.axis_size("lat")
    pairs = []
    for island in range(islands):
        for band in range(bands):
            to_island, to_band = place(island, band)
            pairs.append((island * bands + band, to_island * bands + to_band))
    return lax.ppermute(value, ("dom", "lat"), pairs)


ORDER = ("main", "xa", "xb", "ka", "kb")


def body(states, stir_noise, ancestors):
    islands, bands = lax.axis_size("dom"), lax.axis_size("lat")
    rows, columns = states.shape[2:]
    blocks = columns // LANES
    wide = rows + 2 * HALO
    state_tiles, noise_tiles = row_tiles(states), row_tiles(stir_noise)
    table = jnp.swapaxes(ancestors, 1, 2)

    def pair(band, turn):
        partner = band + 1 if band % 2 == turn else band - 1
        return partner if 0 <= partner < bands else None

    def following(island, band):
        return (island + 1) % islands, band

    def beside(island, band):
        return (island ^ 1 if islands % 2 == 0 else (island + 1) % islands), band

    def across(turn, step):
        def place(island, band):
            partner = pair(band, turn)
            if partner is not None:
                return (island + step) % islands, partner
            return ((island + step) % islands, band) if step else beside(island, band)

        return place

    real = jnp.float32
    full, edge = (VMEM, (4 * rows, blocks, LANES), real), (VMEM, (3 * HALO + NEAR, blocks, LANES), real)
    later_rows = (VMEM, (states.shape[1] * rows, blocks, LANES), real)
    sends = {}
    sends["main"], state_tiles, noise_tiles, table = on_chip(
        functools.partial(collect, islands=islands),
        [HBM] * 3,
        [full, (VMEM, state_tiles.shape, real), (VMEM, noise_tiles.shape, real), (VMEM, table.shape, jnp.int32)],
        [pltpu.SemaphoreType.DMA((4,))],
    )(*(pltpu.with_memory_space_constraint(value, pltpu.HBM) for value in (state_tiles, noise_tiles, table)))
    sends["xa"], sends["xb"], sends["ka"], sends["kb"], kmain, later = on_chip(
        functools.partial(edges, islands=islands), [VMEM] * 3, [edge] * 4 + [full, later_rows]
    )(state_tiles, noise_tiles, table)
    places = {
        "main": following,
        "xa": across(0, 1),
        "xb": across(1, 1),
        "ka": across(0, 0),
        "kb": across(1, 0),
    }
    got = {name: send(sends[name], places[name]) for name in ORDER}
    sources = (table, got["main"], got["xa"], got["xb"], kmain, got["ka"], got["kb"], later)

    work = [pltpu.VMEM((3 * wide, blocks, LANES), real)] * 2 + [pltpu.VMEM((rows + 2 * NEAR, blocks, LANES), real)]
    result = (3,) + state_tiles.shape[2:]
    flops = 60 * wide * columns * 4 * STEPS
    sizes = dict(islands=islands, bands=bands)
    (first,) = on_chip(functools.partial(payload_odd, **sizes), [VMEM] * 8, [(VMEM, result, real)], work, flops)(*sources)
    far = send(first, following)
    (second,) = on_chip(functools.partial(payload_even, **sizes), [VMEM] * 8, [(VMEM, result, real)], work, flops)(*sources)
    near = send(second, beside)
    (third,) = on_chip(functools.partial(keep_local, bands=bands), [VMEM] * 8, [(VMEM, result, real)], work, flops)(
        *sources
    )
    (out,) = on_chip(
        finish, [VMEM] * 5, [(HBM, state_tiles.shape, real)], [pltpu.SemaphoreType.DMA((2,))]
    )(table, far, second, near, third)
    return from_row_tiles(out)


def solution(mesh):
    in_specs = (P(None, "dom", "lat", None), P(None, "dom", "lat", None), P())
    out_specs = P(None, "dom", "lat", None)
    return jax.shard_map(body, mesh=mesh, in_specs=in_specs, out_specs=out_specs, check_vma=False)
```

```python
import functools

import jax
import jax.numpy as jnp
from jax import lax
from jax.experimental import pallas as pl
from jax.experimental.pallas import tpu as pltpu
from jax.sharding import PartitionSpec as P

STEPS = 2
FILTER_ROUNDS = 2

time_step = 0.2
viscosity = 0.05
rotation = 0.3

LANES = 128
TILE = 8
NEAR = 2 * STEPS
HALO = NEAR * FILTER_ROUNDS
VMEM_LIMIT = 16 << 20

diffuse = time_step * viscosity
half = 0.5 * time_step
gravity = half * half
keep = 1.0 - 4.0 * diffuse


def row_tiles(value):
    lead, (rows, columns) = value.shape[:-2], value.shape[-2:]
    blocks = columns // LANES
    value = value.reshape(*lead, rows // TILE, TILE, blocks, LANES)
    return jnp.swapaxes(value, -3, -2).reshape(*lead, rows // TILE, blocks * TILE, LANES)


def from_row_tiles(value):
    lead, (tiles, sublanes) = value.shape[:-3], value.shape[-3:-1]
    blocks = sublanes // TILE
    value = jnp.swapaxes(value.reshape(*lead, tiles, blocks, TILE, LANES), -3, -2)
    return value.reshape(*lead, tiles * TILE, blocks * LANES)


def entries(table, cycle, island):
    lane = lax.broadcasted_iota(jnp.int32, table.shape[2:], 0)[None]
    first, second = (
        jnp.sum(jnp.where(lane == island, table[cycle, slot : slot + 1].astype(jnp.float32), 0.0))
        for slot in range(2)
    )
    return (
        jnp.minimum(first, second).astype(jnp.int32),
        jnp.maximum(first, second).astype(jnp.int32),
        (second > first).astype(jnp.int32),
    )


def collect(state_hbm, noise_hbm, table_hbm, main, state_ref, noise_ref, table_ref, done, *, islands):
    copies = [
        pltpu.make_async_copy(source, target, done.at[index])
        for index, (source, target) in enumerate(
            ((table_hbm, table_ref), (state_hbm, state_ref), (noise_hbm.at[0], noise_ref.at[0]), (noise_hbm.at[1], noise_ref.at[1]))
        )
    ]
    for copy in copies:
        copy.start()
    slots, tiles = state_ref.shape[1], state_ref.shape[2]
    rows = tiles * TILE
    copies[0].wait()
    _, wanted, _ = entries(table_ref[...], 0, lax.rem(lax.axis_index("dom") + 1, islands))
    sent = jnp.clip(wanted - slots, 0, slots - 1)
    copies[1].wait()
    for field in range(3):
        for row in range(rows):
            main[field * rows + row] = state_row(state_ref, field, sent, row // TILE, row % TILE)
    copies[2].wait()
    for row in range(rows):
        main[3 * rows + row] = noise_row(noise_ref, 0, sent, row // TILE, row % TILE)
    copies[3].wait()


def state_row(state_ref, field, slot, tile, row):
    blocks = state_ref.shape[3] // TILE
    value = state_ref[field, slot, tile, pl.ds(row, blocks, stride=TILE), :]
    return value if field == 0 else value * half


def noise_row(noise_ref, cycle, slot, tile, row):
    blocks = noise_ref.shape[3] // TILE
    return noise_ref[cycle, slot, tile, pl.ds(row, blocks, stride=TILE), :]


def edges(state_ref, noise_ref, table_ref, xa, xb, ka, kb, kmain, later, plan, *, islands):
    slots, tiles = state_ref.shape[1], state_ref.shape[2]
    rows = tiles * TILE
    island = lax.axis_index("dom")
    odd = lax.rem(lax.axis_index("lat"), 2)
    table = table_ref[...]
    _, wanted, _ = entries(table, 0, lax.rem(island + 1, islands))
    kept, _, foreign = entries(table, 0, island)
    sent = jnp.clip(wanted - slots, 0, slots - 1)
    kept = jnp.clip(kept, 0, slots - 1)
    _, taken_slot, _ = entries(table, 1, lax.rem(island + 1, islands))
    kept_slot, _, position = entries(table, 1, island)
    for index, value in enumerate((taken_slot - slots == foreign, kept_slot == foreign, position == 1)):
        plan[index] = jnp.full(plan.shape[1:], value.astype(jnp.float32))
    for slot, edge, bottom in ((sent, xa, 1 - odd), (sent, xb, odd), (kept, ka, 1 - odd), (kept, kb, odd)):
        tile = bottom * (tiles - 1)
        for field in range(3):
            for row in range(HALO):
                edge[field * HALO + row] = state_row(state_ref, field, slot, tile, row)
        for row in range(NEAR):
            edge[3 * HALO + row] = noise_row(noise_ref, 0, slot, tile, bottom * (TILE - NEAR) + row)
    for field in range(3):
        for row in range(rows):
            kmain[field * rows + row] = state_row(state_ref, field, kept, row // TILE, row % TILE)
    for row in range(rows):
        kmain[3 * rows + row] = noise_row(noise_ref, 0, kept, row // TILE, row % TILE)
    for index, slot in enumerate((1 - foreign, foreign)):
        for row in range(rows):
            later[index * rows + row] = noise_row(noise_ref, 1, slot, row // TILE, row % TILE)


def tendency_rows(load, store, first, last, coriolis):
    blocks = load(0, first).shape[0]
    lane = lax.broadcasted_iota(jnp.int32, (blocks, LANES), 1)
    at_end, at_start = lane == LANES - 1, lane == 0

    def east(value):
        turned = pltpu.roll(value, LANES - 1, 1)
        return jnp.where(at_end, pltpu.roll(turned, blocks - 1, 0), turned)

    def west(value):
        turned = pltpu.roll(value, 1, 1)
        return jnp.where(at_start, pltpu.roll(turned, 1, 0), turned)

    def column(row):
        h, u, v = (load(field, row) for field in range(3))
        minus, plus = diffuse - v, diffuse + v
        return h, u, v, minus, plus, h * minus - v, h * plus + v

    below, here = column(first - 1), column(first)
    for row in range(first, last):
        above = column(row + 1)
        h, u, v, v_minus, v_plus, _, _ = here
        h_east, h_west, u_east, u_west, v_east, v_west = east(h), west(h), east(u), west(u), east(v), west(v)
        u_minus, u_plus = diffuse - u, diffuse + u
        turn = coriolis(row)
        h_new = (
            (keep * h + (h_east * (diffuse - u_east) - u_east))
            + (h_west * (diffuse + u_west) + u_west)
            + (above[5] + below[6])
        )
        u_new = (
            (keep * u + u_east * u_minus)
            + (u_west * u_plus + above[1] * v_minus)
            + (below[1] * v_plus + turn * v)
            - gravity * (h_east - h_west)
        )
        v_new = (
            (keep * v + v_east * u_minus)
            + (v_west * u_plus + above[2] * v_minus)
            + (below[2] * v_plus - turn * u)
            - gravity * (above[0] - below[0])
        )
        store(row, h_new, u_new, v_new)
        below, here = here, above


def forecast(arrived, sources, out, state, middle, noise, bands):
    main, xa, xb, kmain, ka, kb, later = sources
    rows = main.shape[0] // 4
    blocks = main.shape[1]
    wide = rows + 2 * HALO
    band = lax.axis_index("lat")
    odd = lax.rem(band, 2)
    arrived = arrived > 0.5
    inside_low = (band > 0).astype(jnp.float32)
    inside_high = (band < bands - 1).astype(jnp.float32)

    for field in range(3):
        for row in range(rows):
            place = field * rows + row
            state[field * wide + HALO + row] = jnp.where(arrived, main[place], kmain[place])
    for row in range(rows):
        noise[NEAR + row] = jnp.where(arrived, main[3 * rows + row], kmain[3 * rows + row])
    for first, second, high in ((xa, ka, 1 - odd), (xb, kb, odd)):
        inside = jnp.where(high == 1, inside_high, inside_low)
        start, start_noise = high * (rows + HALO), high * (rows + NEAR)
        for field in range(3):
            for row in range(HALO):
                place = field * HALO + row
                state[field * wide + start + row] = jnp.where(arrived, first[place], second[place]) * inside
        for row in range(NEAR):
            place = 3 * HALO + row
            noise[start_noise + row] = jnp.where(arrived, first[place], second[place]) * inside

    def within(row, value):
        if row < HALO:
            return value * inside_low
        if row >= HALO + rows:
            return value * inside_high
        return value

    start = (band * rows - HALO).astype(jnp.float32)
    slope = time_step * rotation * 2.0 / (rows * bands)
    base = slope * (start + 0.5) - time_step * rotation

    def coriolis(row):
        return base + slope * row

    margin = 0
    for cycle in range(FILTER_ROUNDS):
        for step in range(STEPS):
            last = step == STEPS - 1

            def to_middle(row, *values):
                for field, value in enumerate(values):
                    middle[field * wide + row] = within(row, value)

            def to_state(row, *values, cycle=cycle, last=last):
                final = last and cycle == FILTER_ROUNDS - 1
                for field, value in enumerate(values):
                    value = within(row, 0.5 * (state[field * wide + row] + value))
                    if last and field == 0:
                        if cycle == 0:
                            value = value + noise[row - HALO + NEAR]
                        else:
                            own = row - HALO
                            value = value + jnp.where(arrived, later[rows + own], later[own])
                    if final:
                        own = row - HALO
                        value = value if field == 0 else value * (1.0 / half)
                        out[field, own // TILE, pl.ds(own % TILE, blocks, stride=TILE), :] = value
                    else:
                        state[field * wide + row] = value

            margin += 1
            tendency_rows(lambda field, row: state[field * wide + row], to_middle, margin, wide - margin, coriolis)
            margin += 1
            tendency_rows(lambda field, row: middle[field * wide + row], to_state, margin, wide - margin, coriolis)


def odd_island():
    return lax.rem(lax.axis_index("dom"), 2)


def payload_odd(plan, *refs, bands):
    *sources, out, state, middle, noise = refs

    @pl.when(odd_island() == 1)
    def _():
        forecast(plan[0], sources, out, state, middle, noise, bands)


def payload_even(plan, *refs, bands):
    *sources, out, state, middle, noise = refs
    forecast(plan[odd_island()], sources, out, state, middle, noise, bands)


def keep_local(plan, *refs, bands):
    *sources, out, state, middle, noise = refs

    @pl.when(odd_island() == 0)
    def _():
        forecast(plan[1], sources, out, state, middle, noise, bands)


def finish(plan, far, second, near, third, out, done):
    position = jnp.where(plan[2][0, 0] > 0.5, 1, 0)

    def write(kept, taken):
        copies = [
            pltpu.make_async_copy(kept, out.at[:, 1 - position], done.at[0]),
            pltpu.make_async_copy(taken, out.at[:, position], done.at[1]),
        ]
        for copy in copies:
            copy.start()
        for copy in copies:
            copy.wait()

    @pl.when(odd_island() == 1)
    def _():
        write(second, near)

    @pl.when(odd_island() == 0)
    def _():
        write(third, far)


VMEM = pl.BlockSpec(memory_space=pltpu.VMEM)
HBM = pl.BlockSpec(memory_space=pltpu.HBM)


def on_chip(kernel, ins, outs, scratch=(), flops=0, **more):
    return pl.pallas_call(
        kernel,
        in_specs=ins,
        out_shape=[jax.ShapeDtypeStruct(shape, dtype) for _, shape, dtype in outs],
        out_specs=[spec for spec, _, _ in outs],
        scratch_shapes=scratch,
        cost_estimate=pl.CostEstimate(flops=flops, bytes_accessed=1 << 20, transcendentals=0),
        compiler_params=pltpu.CompilerParams(vmem_limit_bytes=VMEM_LIMIT),
        **more,
    )


def send(value, place):
    islands, bands = lax.axis_size("dom"), lax.axis_size("lat")
    pairs = []
    for island in range(islands):
        for band in range(bands):
            to_island, to_band = place(island, band)
            pairs.append((island * bands + band, to_island * bands + to_band))
    return lax.ppermute(value, ("dom", "lat"), pairs)


ORDER = ("main", "xa", "xb", "ka", "kb")


def body(states, stir_noise, ancestors):
    islands, bands = lax.axis_size("dom"), lax.axis_size("lat")
    rows, columns = states.shape[2:]
    blocks = columns // LANES
    wide = rows + 2 * HALO
    state_tiles, noise_tiles = row_tiles(states), row_tiles(stir_noise)
    table = jnp.swapaxes(ancestors, 1, 2)

    def pair(band, turn):
        partner = band + 1 if band % 2 == turn else band - 1
        return partner if 0 <= partner < bands else None

    def following(island, band):
        return (island + 1) % islands, band

    def beside(island, band):
        return (island ^ 1 if islands % 2 == 0 else (island + 1) % islands), band

    def across(turn, step):
        def place(island, band):
            partner = pair(band, turn)
            if partner is not None:
                return (island + step) % islands, partner
            return ((island + step) % islands, band) if step else beside(island, band)

        return place

    real = jnp.float32
    full, edge = (VMEM, (4 * rows, blocks, LANES), real), (VMEM, (3 * HALO + NEAR, blocks, LANES), real)
    later_rows = (VMEM, (states.shape[1] * rows, blocks, LANES), real)
    sends = {}
    sends["main"], state_tiles, noise_tiles, table = on_chip(
        functools.partial(collect, islands=islands),
        [HBM] * 3,
        [full, (VMEM, state_tiles.shape, real), (VMEM, noise_tiles.shape, real), (VMEM, table.shape, jnp.int32)],
        [pltpu.SemaphoreType.DMA((4,))],
    )(*(pltpu.with_memory_space_constraint(value, pltpu.HBM) for value in (state_tiles, noise_tiles, table)))
    sends["xa"], sends["xb"], sends["ka"], sends["kb"], kmain, later, plan = on_chip(
        functools.partial(edges, islands=islands),
        [VMEM] * 3,
        [edge] * 4 + [full, later_rows, (VMEM, (3, blocks, LANES), real)],
    )(state_tiles, noise_tiles, table)
    places = {
        "main": following,
        "xa": across(0, 1),
        "xb": across(1, 1),
        "ka": across(0, 0),
        "kb": across(1, 0),
    }
    got = {name: send(sends[name], places[name]) for name in ORDER}
    sources = (plan, got["main"], got["xa"], got["xb"], kmain, got["ka"], got["kb"], later)

    work = [pltpu.VMEM((3 * wide, blocks, LANES), real)] * 2 + [pltpu.VMEM((rows + 2 * NEAR, blocks, LANES), real)]
    result = (3,) + state_tiles.shape[2:]
    flops = 60 * wide * columns * 4 * STEPS
    sizes = dict(bands=bands)
    (first,) = on_chip(functools.partial(payload_odd, **sizes), [VMEM] * 8, [(VMEM, result, real)], work, flops)(*sources)
    far = send(first, following)
    (second,) = on_chip(functools.partial(payload_even, **sizes), [VMEM] * 8, [(VMEM, result, real)], work, flops)(*sources)
    near = send(second, beside)
    (third,) = on_chip(functools.partial(keep_local, bands=bands), [VMEM] * 8, [(VMEM, result, real)], work, flops)(
        *sources
    )
    (out,) = on_chip(
        finish, [VMEM] * 5, [(HBM, state_tiles.shape, real)], [pltpu.SemaphoreType.DMA((2,))]
    )(plan, far, second, near, third)
    return from_row_tiles(out)


def solution(mesh):
    in_specs = (P(None, "dom", "lat", None), P(None, "dom", "lat", None), P())
    out_specs = P(None, "dom", "lat", None)
    return jax.shard_map(body, mesh=mesh, in_specs=in_specs, out_specs=out_specs, check_vma=False)
```

```python
import functools

import jax
import jax.numpy as jnp
from jax import lax
from jax.experimental import pallas as pl
from jax.experimental.pallas import tpu as pltpu
from jax.sharding import PartitionSpec as P

STEPS = 2
FILTER_ROUNDS = 2

time_step = 0.2
viscosity = 0.05
rotation = 0.3

LANES = 128
TILE = 8
NEAR = 2 * STEPS
HALO = NEAR * FILTER_ROUNDS
VMEM_LIMIT = 16 << 20

diffuse = time_step * viscosity
half = 0.5 * time_step
gravity = half * half
keep = 1.0 - 4.0 * diffuse


def row_tiles(value):
    lead, (rows, columns) = value.shape[:-2], value.shape[-2:]
    blocks = columns // LANES
    value = value.reshape(*lead, rows // TILE, TILE, blocks, LANES)
    return jnp.swapaxes(value, -3, -2).reshape(*lead, rows // TILE, blocks * TILE, LANES)


def from_row_tiles(value):
    lead, (tiles, sublanes) = value.shape[:-3], value.shape[-3:-1]
    blocks = sublanes // TILE
    value = jnp.swapaxes(value.reshape(*lead, tiles, blocks, TILE, LANES), -3, -2)
    return value.reshape(*lead, tiles * TILE, blocks * LANES)


def entries(table, cycle, island):
    lane = lax.broadcasted_iota(jnp.int32, table.shape[2:], 0)[None]
    first, second = (
        jnp.sum(jnp.where(lane == island, table[cycle, slot : slot + 1].astype(jnp.float32), 0.0))
        for slot in range(2)
    )
    return (
        jnp.minimum(first, second).astype(jnp.int32),
        jnp.maximum(first, second).astype(jnp.int32),
        (second > first).astype(jnp.int32),
    )


def collect(state_hbm, noise_hbm, table_hbm, main, state_ref, noise_ref, table_ref, done, *, islands):
    copies = [
        pltpu.make_async_copy(source, target, done.at[index])
        for index, (source, target) in enumerate(
            ((table_hbm, table_ref), (state_hbm, state_ref), (noise_hbm.at[0], noise_ref.at[0]), (noise_hbm.at[1], noise_ref.at[1]))
        )
    ]
    for copy in copies:
        copy.start()
    slots, tiles = state_ref.shape[1], state_ref.shape[2]
    rows = tiles * TILE
    copies[0].wait()
    _, wanted, _ = entries(table_ref[...], 0, lax.rem(lax.axis_index("dom") + 1, islands))
    sent = jnp.clip(wanted - slots, 0, slots - 1)
    copies[1].wait()
    for field in range(3):
        for row in range(rows):
            main[field * rows + row] = state_row(state_ref, field, sent, row // TILE, row % TILE)
    copies[2].wait()
    for row in range(rows):
        main[3 * rows + row] = noise_row(noise_ref, 0, sent, row // TILE, row % TILE)
    copies[3].wait()


def state_row(state_ref, field, slot, tile, row):
    blocks = state_ref.shape[3] // TILE
    value = state_ref[field, slot, tile, pl.ds(row, blocks, stride=TILE), :]
    return value if field == 0 else value * half


def noise_row(noise_ref, cycle, slot, tile, row):
    blocks = noise_ref.shape[3] // TILE
    return noise_ref[cycle, slot, tile, pl.ds(row, blocks, stride=TILE), :]


def edges(state_ref, noise_ref, table_ref, xa, xb, ka, kb, kmain, later, plan, *, islands):
    slots, tiles = state_ref.shape[1], state_ref.shape[2]
    rows = tiles * TILE
    island = lax.axis_index("dom")
    odd = lax.rem(lax.axis_index("lat"), 2)
    table = table_ref[...]
    _, wanted, _ = entries(table, 0, lax.rem(island + 1, islands))
    kept, _, foreign = entries(table, 0, island)
    sent = jnp.clip(wanted - slots, 0, slots - 1)
    kept = jnp.clip(kept, 0, slots - 1)
    _, taken_slot, _ = entries(table, 1, lax.rem(island + 1, islands))
    kept_slot, _, position = entries(table, 1, island)
    for index, value in enumerate((taken_slot - slots == foreign, kept_slot == foreign, position == 1)):
        plan[index] = jnp.full(plan.shape[1:], value.astype(jnp.float32))
    for slot, edge, bottom in ((sent, xa, 1 - odd), (sent, xb, odd), (kept, ka, 1 - odd), (kept, kb, odd)):
        tile = bottom * (tiles - 1)
        for field in range(3):
            for row in range(HALO):
                edge[field * HALO + row] = state_row(state_ref, field, slot, tile, row)
        for row in range(NEAR):
            edge[3 * HALO + row] = noise_row(noise_ref, 0, slot, tile, bottom * (TILE - NEAR) + row)
    for field in range(3):
        for row in range(rows):
            kmain[field * rows + row] = state_row(state_ref, field, kept, row // TILE, row % TILE)
    for row in range(rows):
        kmain[3 * rows + row] = noise_row(noise_ref, 0, kept, row // TILE, row % TILE)
    for index, slot in enumerate((1 - foreign, foreign)):
        for row in range(rows):
            later[index * rows + row] = noise_row(noise_ref, 1, slot, row // TILE, row % TILE)


def tendency_rows(load, store, first, last, coriolis):
    blocks = load(0, first).shape[0]
    lane = lax.broadcasted_iota(jnp.int32, (blocks, LANES), 1)
    at_end, at_start = lane == LANES - 1, lane == 0

    def east(value):
        turned = pltpu.roll(value, LANES - 1, 1)
        return jnp.where(at_end, pltpu.roll(turned, blocks - 1, 0), turned)

    def west(value):
        turned = pltpu.roll(value, 1, 1)
        return jnp.where(at_start, pltpu.roll(turned, 1, 0), turned)

    def column(row):
        h, u, v = (load(field, row) for field in range(3))
        minus, plus = diffuse - v, diffuse + v
        return h, u, v, minus, plus, h * minus - v, h * plus + v

    below, here = column(first - 1), column(first)
    for row in range(first, last):
        above = column(row + 1)
        h, u, v, v_minus, v_plus, _, _ = here
        h_east, h_west, u_east, u_west, v_east, v_west = east(h), west(h), east(u), west(u), east(v), west(v)
        u_minus, u_plus = diffuse - u, diffuse + u
        turn = coriolis(row)
        h_new = (
            (keep * h + (h_east * (diffuse - u_east) - u_east))
            + (h_west * (diffuse + u_west) + u_west)
            + (above[5] + below[6])
        )
        u_new = (
            (keep * u + u_east * u_minus)
            + (u_west * u_plus + above[1] * v_minus)
            + (below[1] * v_plus + turn * v)
            - gravity * (h_east - h_west)
        )
        v_new = (
            (keep * v + v_east * u_minus)
            + (v_west * u_plus + above[2] * v_minus)
            + (below[2] * v_plus - turn * u)
            - gravity * (above[0] - below[0])
        )
        store(row, h_new, u_new, v_new)
        below, here = here, above


def forecast(arrived, sources, out, state, middle, noise, bands):
    main, xa, xb, kmain, ka, kb, later = sources
    rows = main.shape[0] // 4
    blocks = main.shape[1]
    wide = rows + 2 * HALO
    band = lax.axis_index("lat")
    odd = lax.rem(band, 2)
    arrived = arrived > 0.5
    inside_low = (band > 0).astype(jnp.float32)
    inside_high = (band < bands - 1).astype(jnp.float32)

    for field in range(3):
        for row in range(rows):
            place = field * rows + row
            state[field * wide + HALO + row] = jnp.where(arrived, main[place], kmain[place])
    for row in range(rows):
        noise[NEAR + row] = jnp.where(arrived, main[3 * rows + row], kmain[3 * rows + row])
    for first, second, high in ((xa, ka, 1 - odd), (xb, kb, odd)):
        inside = jnp.where(high == 1, inside_high, inside_low)
        start, start_noise = high * (rows + HALO), high * (rows + NEAR)
        for field in range(3):
            for row in range(HALO):
                place = field * HALO + row
                state[field * wide + start + row] = jnp.where(arrived, first[place], second[place]) * inside
        for row in range(NEAR):
            place = 3 * HALO + row
            noise[start_noise + row] = jnp.where(arrived, first[place], second[place]) * inside

    def within(row, value):
        if row < HALO:
            return value * inside_low
        if row >= HALO + rows:
            return value * inside_high
        return value

    start = (band * rows - HALO).astype(jnp.float32)
    slope = time_step * rotation * 2.0 / (rows * bands)
    base = slope * (start + 0.5) - time_step * rotation

    def coriolis(row):
        return base + slope * row

    margin = 0
    for cycle in range(FILTER_ROUNDS):
        for step in range(STEPS):
            last = step == STEPS - 1

            def to_middle(row, *values):
                for field, value in enumerate(values):
                    middle[field * wide + row] = within(row, value)

            def to_state(row, *values, cycle=cycle, last=last):
                final = last and cycle == FILTER_ROUNDS - 1
                for field, value in enumerate(values):
                    value = within(row, 0.5 * (state[field * wide + row] + value))
                    if last and field == 0:
                        if cycle == 0:
                            value = value + noise[row - HALO + NEAR]
                        else:
                            own = row - HALO
                            value = value + jnp.where(arrived, later[rows + own], later[own])
                    if final:
                        own = row - HALO
                        value = value if field == 0 else value * (1.0 / half)
                        out[field, own // TILE, pl.ds(own % TILE, blocks, stride=TILE), :] = value
                    else:
                        state[field * wide + row] = value

            margin += 1
            tendency_rows(lambda field, row: state[field * wide + row], to_middle, margin, wide - margin, coriolis)
            margin += 1
            tendency_rows(lambda field, row: middle[field * wide + row], to_state, margin, wide - margin, coriolis)


def odd_island():
    return lax.rem(lax.axis_index("dom"), 2)


def each_stage():
    for cycle in range(FILTER_ROUNDS):
        for step in range(STEPS):
            stage = 2 * (cycle * STEPS + step) + 1
            yield stage, False, False
            yield stage + 1, True, step == STEPS - 1


def coriolis_of(rows, bands):
    start = (lax.axis_index("lat") * rows - HALO).astype(jnp.float32)
    slope = time_step * rotation * 2.0 / (rows * bands)
    base = slope * (start + 0.5) - time_step * rotation
    return lambda row: base + slope * row


def inner(plan, main, kmain, xa, xb, out, *, bands):
    @pl.when(odd_island() == 1)
    def _():
        rows = kmain.shape[0] // 4
        coriolis = coriolis_of(rows, bands)
        arrived = plan[0] > 0.5

        def place(stage, field, row):
            return (stage * 3 + field) * rows + row - HALO

        noise = 3 * HALO * rows
        for row in range(3 * rows):
            out[row] = jnp.where(arrived, main[row], kmain[row])
        for row in range(rows):
            out[noise + row] = jnp.where(arrived, main[3 * rows + row], kmain[3 * rows + row])
        for stage, ends_step, ends_cycle in each_stage():
            if stage == HALO:
                break

            def store(row, *values, stage=stage, ends_step=ends_step, ends_cycle=ends_cycle):
                for field, value in enumerate(values):
                    if ends_step:
                        value = 0.5 * (out[place(stage - 2, field, row)] + value)
                    if ends_cycle and field == 0:
                        value = value + out[noise + row - HALO]
                    out[place(stage, field, row)] = value

            def load(field, row, stage=stage):
                return out[place(stage - 1, field, row)]

            tendency_rows(load, store, HALO + stage, HALO + rows - stage, coriolis)


def outer(plan, inside, xa, xb, ka, kb, later, out, work, noise, *, bands):
    @pl.when(odd_island() == 1)
    def _():
        rows = out.shape[1] * TILE
        blocks = inside.shape[1]
        band = lax.axis_index("lat")
        odd = lax.rem(band, 2)
        arrived = plan[0] > 0.5
        coriolis = coriolis_of(rows, bands)
        inner_side = ((band > 0).astype(jnp.float32), (band < bands - 1).astype(jnp.float32))
        size = 3 * HALO * HALO

        for first, second, high in ((xa, ka, 1 - odd), (xb, kb, odd)):
            keep_rows = jnp.where(high == 1, inner_side[1], inner_side[0])
            for row in range(3 * HALO):
                work[high * size + row] = jnp.where(arrived, first[row], second[row]) * keep_rows
            for row in range(NEAR):
                place = 3 * HALO + row
                noise[high * NEAR + row] = jnp.where(arrived, first[place], second[place]) * keep_rows

        def first_row(side, stage):
            return HALO + rows - stage if side else stage

        def outside(row):
            return row < HALO or row >= HALO + rows

        def load(side, stage, field, row):
            local = row - first_row(side, stage)
            if 0 <= local < HALO:
                return work[side * size + (stage * 3 + field) * HALO + local]
            return inside[(stage * 3 + field) * rows + row - HALO]

        for stage, ends_step, ends_cycle in each_stage():
            for side in range(2):

                def store(row, *values, stage=stage, side=side, ends_step=ends_step, ends_cycle=ends_cycle):
                    own = row - HALO
                    for field, value in enumerate(values):
                        if ends_step:
                            value = 0.5 * (load(side, stage - 2, field, row) + value)
                        if stage == HALO:
                            if field == 0:
                                value = value + jnp.where(arrived, later[rows + own], later[own])
                            else:
                                value = value * (1.0 / half)
                            out[field, own // TILE, pl.ds(own % TILE, blocks, stride=TILE), :] = value
                            continue
                        if ends_cycle and field == 0:
                            if outside(row):
                                value = value + noise[side * NEAR + (own - rows if side else own + NEAR)]
                            else:
                                value = value + inside[3 * HALO * rows + own]
                        if outside(row):
                            value = value * inner_side[side]
                        work[side * size + (stage * 3 + field) * HALO + row - first_row(side, stage)] = value

                start = first_row(side, stage)
                tendency_rows(
                    lambda field, row, stage=stage, side=side: load(side, stage - 1, field, row),
                    store,
                    start,
                    start + HALO,
                    coriolis,
                )


def payload_even(plan, *refs, bands):
    main, xa, xb, kmain, ka, kb, kc, later, out, state, middle, noise = refs

    @pl.when(odd_island() == 1)
    def _():
        forecast(plan[1], (main, xa, xb, kmain, ka, kb, later), out, state, middle, noise, bands)

    @pl.when(odd_island() == 0)
    def _():
        forecast(plan[0], (main, xa, xb, kmain, ka, kc, later), out, state, middle, noise, bands)


def keep_local(plan, *refs, bands):
    main, xa, xb, kmain, ka, _, kc, later, out, state, middle, noise = refs
    sources = main, xa, xb, kmain, ka, kc, later

    @pl.when(odd_island() == 0)
    def _():
        forecast(plan[1], sources, out, state, middle, noise, bands)


def finish(plan, far, second, near, third, out, done):
    position = jnp.where(plan[2][0, 0] > 0.5, 1, 0)

    def write(kept, taken):
        copies = [
            pltpu.make_async_copy(kept, out.at[:, 1 - position], done.at[0]),
            pltpu.make_async_copy(taken, out.at[:, position], done.at[1]),
        ]
        for copy in copies:
            copy.start()
        for copy in copies:
            copy.wait()

    @pl.when(odd_island() == 1)
    def _():
        write(second, near)

    @pl.when(odd_island() == 0)
    def _():
        write(third, far)


VMEM = pl.BlockSpec(memory_space=pltpu.VMEM)
HBM = pl.BlockSpec(memory_space=pltpu.HBM)


def on_chip(kernel, ins, outs, scratch=(), flops=0, **more):
    return pl.pallas_call(
        kernel,
        in_specs=ins,
        out_shape=[jax.ShapeDtypeStruct(shape, dtype) for _, shape, dtype in outs],
        out_specs=[spec for spec, _, _ in outs],
        scratch_shapes=scratch,
        cost_estimate=pl.CostEstimate(flops=flops, bytes_accessed=1 << 20, transcendentals=0),
        compiler_params=pltpu.CompilerParams(vmem_limit_bytes=VMEM_LIMIT),
        **more,
    )


def send(value, place):
    islands, bands = lax.axis_size("dom"), lax.axis_size("lat")
    pairs = []
    for island in range(islands):
        for band in range(bands):
            to_island, to_band = place(island, band)
            pairs.append((island * bands + band, to_island * bands + to_band))
    return lax.ppermute(value, ("dom", "lat"), pairs)


ORDER = ("main", "xa", "xb", "ka", "kb", "kc")


def body(states, stir_noise, ancestors):
    islands, bands = lax.axis_size("dom"), lax.axis_size("lat")
    rows, columns = states.shape[2:]
    blocks = columns // LANES
    wide = rows + 2 * HALO
    state_tiles, noise_tiles = row_tiles(states), row_tiles(stir_noise)
    table = jnp.swapaxes(ancestors, 1, 2)

    def pair(band, turn):
        partner = band + 1 if band % 2 == turn else band - 1
        return partner if 0 <= partner < bands else None

    def following(island, band):
        return (island + 1) % islands, band

    def beside(island, band):
        return (island ^ 1 if islands % 2 == 0 else (island + 1) % islands), band

    def across(turn, step):
        def place(island, band):
            partner = pair(band, turn)
            if partner is not None:
                return (island + step) % islands, partner
            return ((island + step) % islands, band) if step else beside(island, band)

        return place

    def only(parity):
        def place(island, band):
            partner = pair(band, 1)
            if partner is None:
                return beside(island, band)
            if island % 2 == parity:
                return island, partner
            return (island + 2) % islands, band

        return place

    real = jnp.float32
    full, edge = (VMEM, (4 * rows, blocks, LANES), real), (VMEM, (3 * HALO + NEAR, blocks, LANES), real)
    later_rows = (VMEM, (states.shape[1] * rows, blocks, LANES), real)
    sends = {}
    sends["main"], state_tiles, noise_tiles, table = on_chip(
        functools.partial(collect, islands=islands),
        [HBM] * 3,
        [full, (VMEM, state_tiles.shape, real), (VMEM, noise_tiles.shape, real), (VMEM, table.shape, jnp.int32)],
        [pltpu.SemaphoreType.DMA((4,))],
    )(*(pltpu.with_memory_space_constraint(value, pltpu.HBM) for value in (state_tiles, noise_tiles, table)))
    sends["xa"], sends["xb"], sends["ka"], sends["kb"], kmain, later, plan = on_chip(
        functools.partial(edges, islands=islands),
        [VMEM] * 3,
        [edge] * 4 + [full, later_rows, (VMEM, (3, blocks, LANES), real)],
    )(state_tiles, noise_tiles, table)
    places = {
        "main": following,
        "xa": across(0, 1),
        "xb": across(1, 1),
        "ka": across(0, 0),
        "kb": only(1),
        "kc": only(0),
    }
    sends["kc"] = sends["kb"]
    got = {name: send(sends[name], places[name]) for name in ORDER}
    late_sources = (plan, got["main"], got["xa"], got["xb"], kmain, got["ka"], got["kb"], got["kc"], later)

    work = [pltpu.VMEM((3 * wide, blocks, LANES), real)] * 2 + [pltpu.VMEM((rows + 2 * NEAR, blocks, LANES), real)]
    result = (3,) + state_tiles.shape[2:]
    flops = 60 * wide * columns * 4 * STEPS
    sizes = dict(bands=bands)
    (inside,) = on_chip(
        functools.partial(inner, **sizes),
        [VMEM] * 5,
        [(VMEM, ((3 * HALO + 1) * rows, blocks, LANES), real)],
    )(plan, got["main"], kmain, got["xa"], got["xb"])
    (first,) = on_chip(
        functools.partial(outer, **sizes),
        [VMEM] * 7,
        [(VMEM, result, real)],
        [pltpu.VMEM((6 * HALO * HALO, blocks, LANES), real), pltpu.VMEM((2 * NEAR, blocks, LANES), real)],
    )(plan, inside, got["xa"], got["xb"], got["ka"], got["kb"], later)
    far = send(first, following)
    (second,) = on_chip(functools.partial(payload_even, **sizes), [VMEM] * 9, [(VMEM, result, real)], work, flops)(*late_sources)
    near = send(second, beside)
    (third,) = on_chip(functools.partial(keep_local, bands=bands), [VMEM] * 9, [(VMEM, result, real)], work, flops)(
        *late_sources
    )
    (out,) = on_chip(
        finish, [VMEM] * 5, [(HBM, state_tiles.shape, real)], [pltpu.SemaphoreType.DMA((2,))]
    )(plan, far, second, near, third)
    return from_row_tiles(out)


def solution(mesh):
    in_specs = (P(None, "dom", "lat", None), P(None, "dom", "lat", None), P())
    out_specs = P(None, "dom", "lat", None)
    return jax.shard_map(body, mesh=mesh, in_specs=in_specs, out_specs=out_specs, check_vma=False)
```

```python
import functools

import jax
import jax.numpy as jnp
from jax import lax
from jax.experimental import pallas as pl
from jax.experimental.pallas import tpu as pltpu
from jax.sharding import PartitionSpec as P

STEPS = 2
FILTER_ROUNDS = 2

time_step = 0.2
viscosity = 0.05
rotation = 0.3

LANES = 128
TILE = 8
NEAR = 2 * STEPS
HALO = NEAR * FILTER_ROUNDS
VMEM_LIMIT = 16 << 20

diffuse = time_step * viscosity
half = 0.5 * time_step
gravity = half * half
keep = 1.0 - 4.0 * diffuse


def row_tiles(value):
    lead, (rows, columns) = value.shape[:-2], value.shape[-2:]
    blocks = columns // LANES
    value = value.reshape(*lead, rows // TILE, TILE, blocks, LANES)
    return jnp.swapaxes(value, -3, -2).reshape(*lead, rows // TILE, blocks * TILE, LANES)


def from_row_tiles(value):
    lead, (tiles, sublanes) = value.shape[:-3], value.shape[-3:-1]
    blocks = sublanes // TILE
    value = jnp.swapaxes(value.reshape(*lead, tiles, blocks, TILE, LANES), -3, -2)
    return value.reshape(*lead, tiles * TILE, blocks * LANES)


def entries(table, cycle, island):
    lane = lax.broadcasted_iota(jnp.int32, table.shape[2:], 0)[None]
    first, second = (
        jnp.sum(jnp.where(lane == island, table[cycle, slot : slot + 1].astype(jnp.float32), 0.0))
        for slot in range(2)
    )
    return (
        jnp.minimum(first, second).astype(jnp.int32),
        jnp.maximum(first, second).astype(jnp.int32),
        (second > first).astype(jnp.int32),
    )


def collect(state_hbm, noise_hbm, table_hbm, main, state_ref, noise_ref, table_ref, done, *, islands):
    copies = [
        pltpu.make_async_copy(source, target, done.at[index])
        for index, (source, target) in enumerate(
            ((table_hbm, table_ref), (state_hbm, state_ref), (noise_hbm.at[0], noise_ref.at[0]), (noise_hbm.at[1], noise_ref.at[1]))
        )
    ]
    for copy in copies:
        copy.start()
    slots, tiles = state_ref.shape[1], state_ref.shape[2]
    rows = tiles * TILE
    copies[0].wait()
    _, wanted, _ = entries(table_ref[...], 0, lax.rem(lax.axis_index("dom") + 1, islands))
    sent = jnp.clip(wanted - slots, 0, slots - 1)
    copies[1].wait()
    for field in range(3):
        for row in range(rows):
            main[field * rows + row] = state_row(state_ref, field, sent, row // TILE, row % TILE)
    copies[2].wait()
    for row in range(rows):
        main[3 * rows + row] = noise_row(noise_ref, 0, sent, row // TILE, row % TILE)
    copies[3].wait()


def state_row(state_ref, field, slot, tile, row):
    blocks = state_ref.shape[3] // TILE
    value = state_ref[field, slot, tile, pl.ds(row, blocks, stride=TILE), :]
    return value if field == 0 else value * half


def noise_row(noise_ref, cycle, slot, tile, row):
    blocks = noise_ref.shape[3] // TILE
    return noise_ref[cycle, slot, tile, pl.ds(row, blocks, stride=TILE), :]


def edges(state_ref, noise_ref, table_ref, xa, xb, ka, kb, kmain, later, plan, *, islands):
    slots, tiles = state_ref.shape[1], state_ref.shape[2]
    rows = tiles * TILE
    island = lax.axis_index("dom")
    odd = lax.rem(lax.axis_index("lat"), 2)
    table = table_ref[...]
    _, wanted, _ = entries(table, 0, lax.rem(island + 1, islands))
    kept, _, foreign = entries(table, 0, island)
    sent = jnp.clip(wanted - slots, 0, slots - 1)
    kept = jnp.clip(kept, 0, slots - 1)
    _, taken_slot, _ = entries(table, 1, lax.rem(island + 1, islands))
    kept_slot, _, position = entries(table, 1, island)
    for index, value in enumerate((taken_slot - slots == foreign, kept_slot == foreign, position == 1)):
        plan[index] = jnp.full(plan.shape[1:], value.astype(jnp.float32))
    for slot, edge, bottom in ((sent, xa, 1 - odd), (sent, xb, odd), (kept, ka, 1 - odd), (kept, kb, odd)):
        tile = bottom * (tiles - 1)
        for field in range(3):
            for row in range(HALO):
                edge[field * HALO + row] = state_row(state_ref, field, slot, tile, row)
        for row in range(NEAR):
            edge[3 * HALO + row] = noise_row(noise_ref, 0, slot, tile, bottom * (TILE - NEAR) + row)
    for field in range(3):
        for row in range(rows):
            kmain[field * rows + row] = state_row(state_ref, field, kept, row // TILE, row % TILE)
    for row in range(rows):
        kmain[3 * rows + row] = noise_row(noise_ref, 0, kept, row // TILE, row % TILE)
    for index, slot in enumerate((1 - foreign, foreign)):
        for row in range(rows):
            later[index * rows + row] = noise_row(noise_ref, 1, slot, row // TILE, row % TILE)


def tendency_rows(load, store, first, last, coriolis):
    for _ in row_steps(load, store, first, last, coriolis):
        pass


def row_steps(load, store, first, last, coriolis):
    blocks = load(0, first).shape[0]
    lane = lax.broadcasted_iota(jnp.int32, (blocks, LANES), 1)
    at_end, at_start = lane == LANES - 1, lane == 0

    def east(value):
        turned = pltpu.roll(value, LANES - 1, 1)
        return jnp.where(at_end, pltpu.roll(turned, blocks - 1, 0), turned)

    def west(value):
        turned = pltpu.roll(value, 1, 1)
        return jnp.where(at_start, pltpu.roll(turned, 1, 0), turned)

    def column(row):
        h, u, v = (load(field, row) for field in range(3))
        minus, plus = diffuse - v, diffuse + v
        return h, u, v, minus, plus, h * minus - v, h * plus + v

    below, here = column(first - 1), column(first)
    for row in range(first, last):
        above = column(row + 1)
        h, u, v, v_minus, v_plus, _, _ = here
        h_east, h_west, u_east, u_west, v_east, v_west = east(h), west(h), east(u), west(u), east(v), west(v)
        u_minus, u_plus = diffuse - u, diffuse + u
        turn = coriolis(row)
        h_new = (
            (keep * h + (h_east * (diffuse - u_east) - u_east))
            + (h_west * (diffuse + u_west) + u_west)
            + (above[5] + below[6])
        )
        u_new = (
            (keep * u + u_east * u_minus)
            + (u_west * u_plus + above[1] * v_minus)
            + (below[1] * v_plus + turn * v)
            - gravity * (h_east - h_west)
        )
        v_new = (
            (keep * v + v_east * u_minus)
            + (v_west * u_plus + above[2] * v_minus)
            + (below[2] * v_plus - turn * u)
            - gravity * (above[0] - below[0])
        )
        store(row, h_new, u_new, v_new)
        below, here = here, above
        yield row


def forecast(arrived, sources, out, state, middle, noise, bands):
    main, xa, xb, kmain, ka, kb, later = sources
    rows = main.shape[0] // 4
    blocks = main.shape[1]
    wide = rows + 2 * HALO
    band = lax.axis_index("lat")
    odd = lax.rem(band, 2)
    arrived = arrived > 0.5
    inside_low = (band > 0).astype(jnp.float32)
    inside_high = (band < bands - 1).astype(jnp.float32)

    for field in range(3):
        for row in range(rows):
            place = field * rows + row
            state[field * wide + HALO + row] = jnp.where(arrived, main[place], kmain[place])
    for row in range(rows):
        noise[NEAR + row] = jnp.where(arrived, main[3 * rows + row], kmain[3 * rows + row])
    for first, second, high in ((xa, ka, 1 - odd), (xb, kb, odd)):
        inside = jnp.where(high == 1, inside_high, inside_low)
        start, start_noise = high * (rows + HALO), high * (rows + NEAR)
        for field in range(3):
            for row in range(HALO):
                place = field * HALO + row
                state[field * wide + start + row] = jnp.where(arrived, first[place], second[place]) * inside
        for row in range(NEAR):
            place = 3 * HALO + row
            noise[start_noise + row] = jnp.where(arrived, first[place], second[place]) * inside

    def within(row, value):
        if row < HALO:
            return value * inside_low
        if row >= HALO + rows:
            return value * inside_high
        return value

    start = (band * rows - HALO).astype(jnp.float32)
    slope = time_step * rotation * 2.0 / (rows * bands)
    base = slope * (start + 0.5) - time_step * rotation

    def coriolis(row):
        return base + slope * row

    margin = 0
    for cycle in range(FILTER_ROUNDS):
        for step in range(STEPS):
            last = step == STEPS - 1

            def to_middle(row, *values):
                for field, value in enumerate(values):
                    middle[field * wide + row] = within(row, value)

            def to_state(row, *values, cycle=cycle, last=last):
                final = last and cycle == FILTER_ROUNDS - 1
                for field, value in enumerate(values):
                    value = within(row, 0.5 * (state[field * wide + row] + value))
                    if last and field == 0:
                        if cycle == 0:
                            value = value + noise[row - HALO + NEAR]
                        else:
                            own = row - HALO
                            value = value + jnp.where(arrived, later[rows + own], later[own])
                    if final:
                        own = row - HALO
                        value = value if field == 0 else value * (1.0 / half)
                        out[field, own // TILE, pl.ds(own % TILE, blocks, stride=TILE), :] = value
                    else:
                        state[field * wide + row] = value

            margin += 1
            tendency_rows(lambda field, row: state[field * wide + row], to_middle, margin, wide - margin, coriolis)
            margin += 1
            tendency_rows(lambda field, row: middle[field * wide + row], to_state, margin, wide - margin, coriolis)


def odd_island():
    return lax.rem(lax.axis_index("dom"), 2)


def each_stage():
    for cycle in range(FILTER_ROUNDS):
        for step in range(STEPS):
            stage = 2 * (cycle * STEPS + step) + 1
            yield stage, False, False
            yield stage + 1, True, step == STEPS - 1


def coriolis_of(rows, bands):
    start = (lax.axis_index("lat") * rows - HALO).astype(jnp.float32)
    slope = time_step * rotation * 2.0 / (rows * bands)
    base = slope * (start + 0.5) - time_step * rotation
    return lambda row: base + slope * row


def inner(plan, main, kmain, xa, xb, out, *, bands):
    @pl.when(odd_island() == 1)
    def _():
        rows = kmain.shape[0] // 4
        coriolis = coriolis_of(rows, bands)
        arrived = plan[0] > 0.5

        def place(stage, field, row):
            return (stage * 3 + field) * rows + row - HALO

        noise = 3 * HALO * rows
        for row in range(3 * rows):
            out[row] = jnp.where(arrived, main[row], kmain[row])
        for row in range(rows):
            out[noise + row] = jnp.where(arrived, main[3 * rows + row], kmain[3 * rows + row])
        for stage, ends_step, ends_cycle in each_stage():
            if stage == HALO:
                break

            def store(row, *values, stage=stage, ends_step=ends_step, ends_cycle=ends_cycle):
                for field, value in enumerate(values):
                    if ends_step:
                        value = 0.5 * (out[place(stage - 2, field, row)] + value)
                    if ends_cycle and field == 0:
                        value = value + out[noise + row - HALO]
                    out[place(stage, field, row)] = value

            def load(field, row, stage=stage):
                return out[place(stage - 1, field, row)]

            tendency_rows(load, store, HALO + stage, HALO + rows - stage, coriolis)


def outer(plan, inside, xa, xb, ka, kb, later, out, work, noise, *, bands):
    @pl.when(odd_island() == 1)
    def _():
        rows = out.shape[1] * TILE
        blocks = inside.shape[1]
        band = lax.axis_index("lat")
        odd = lax.rem(band, 2)
        arrived = plan[0] > 0.5
        coriolis = coriolis_of(rows, bands)
        inner_side = ((band > 0).astype(jnp.float32), (band < bands - 1).astype(jnp.float32))
        size = 3 * HALO * HALO

        for first, second, high in ((xa, ka, 1 - odd), (xb, kb, odd)):
            keep_rows = jnp.where(high == 1, inner_side[1], inner_side[0])
            for row in range(3 * HALO):
                work[high * size + row] = jnp.where(arrived, first[row], second[row]) * keep_rows
            for row in range(NEAR):
                place = 3 * HALO + row
                noise[high * NEAR + row] = jnp.where(arrived, first[place], second[place]) * keep_rows

        def first_row(side, stage):
            return HALO + rows - stage if side else stage

        def outside(row):
            return row < HALO or row >= HALO + rows

        def load(side, stage, field, row):
            local = row - first_row(side, stage)
            if 0 <= local < HALO:
                return work[side * size + (stage * 3 + field) * HALO + local]
            return inside[(stage * 3 + field) * rows + row - HALO]

        for stage, ends_step, ends_cycle in each_stage():
            steps = []
            for side in range(2):

                def store(row, *values, stage=stage, side=side, ends_step=ends_step, ends_cycle=ends_cycle):
                    own = row - HALO
                    for field, value in enumerate(values):
                        if ends_step:
                            value = 0.5 * (load(side, stage - 2, field, row) + value)
                        if stage == HALO:
                            if field == 0:
                                value = value + jnp.where(arrived, later[rows + own], later[own])
                            else:
                                value = value * (1.0 / half)
                            out[field, own // TILE, pl.ds(own % TILE, blocks, stride=TILE), :] = value
                            continue
                        if ends_cycle and field == 0:
                            if outside(row):
                                value = value + noise[side * NEAR + (own - rows if side else own + NEAR)]
                            else:
                                value = value + inside[3 * HALO * rows + own]
                        if outside(row):
                            value = value * inner_side[side]
                        work[side * size + (stage * 3 + field) * HALO + row - first_row(side, stage)] = value

                start = first_row(side, stage)
                steps.append(
                    row_steps(
                        lambda field, row, stage=stage, side=side: load(side, stage - 1, field, row),
                        store,
                        start,
                        start + HALO,
                        coriolis,
                    )
                )
            for _ in zip(*steps, strict=True):
                pass


def payload_even(plan, *refs, bands):
    main, xa, xb, kmain, ka, kb, kc, later, out, state, middle, noise = refs

    @pl.when(odd_island() == 1)
    def _():
        forecast(plan[1], (main, xa, xb, kmain, ka, kb, later), out, state, middle, noise, bands)

    @pl.when(odd_island() == 0)
    def _():
        forecast(plan[0], (main, xa, xb, kmain, ka, kc, later), out, state, middle, noise, bands)


def keep_local(plan, *refs, bands):
    main, xa, xb, kmain, ka, _, kc, later, out, state, middle, noise = refs
    sources = main, xa, xb, kmain, ka, kc, later

    @pl.when(odd_island() == 0)
    def _():
        forecast(plan[1], sources, out, state, middle, noise, bands)


def finish(plan, far, second, near, third, out, done):
    position = jnp.where(plan[2][0, 0] > 0.5, 1, 0)

    def write(kept, taken):
        copies = [
            pltpu.make_async_copy(kept, out.at[:, 1 - position], done.at[0]),
            pltpu.make_async_copy(taken, out.at[:, position], done.at[1]),
        ]
        for copy in copies:
            copy.start()
        for copy in copies:
            copy.wait()

    @pl.when(odd_island() == 1)
    def _():
        write(second, near)

    @pl.when(odd_island() == 0)
    def _():
        write(third, far)


VMEM = pl.BlockSpec(memory_space=pltpu.VMEM)
HBM = pl.BlockSpec(memory_space=pltpu.HBM)


def on_chip(kernel, ins, outs, scratch=(), flops=0, **more):
    return pl.pallas_call(
        kernel,
        in_specs=ins,
        out_shape=[jax.ShapeDtypeStruct(shape, dtype) for _, shape, dtype in outs],
        out_specs=[spec for spec, _, _ in outs],
        scratch_shapes=scratch,
        cost_estimate=pl.CostEstimate(flops=flops, bytes_accessed=1 << 20, transcendentals=0),
        compiler_params=pltpu.CompilerParams(vmem_limit_bytes=VMEM_LIMIT),
        **more,
    )


def send(value, place):
    islands, bands = lax.axis_size("dom"), lax.axis_size("lat")
    pairs = []
    for island in range(islands):
        for band in range(bands):
            to_island, to_band = place(island, band)
            pairs.append((island * bands + band, to_island * bands + to_band))
    return lax.ppermute(value, ("dom", "lat"), pairs)


ORDER = ("main", "xa", "xb", "ka", "kb", "kc")


def body(states, stir_noise, ancestors):
    islands, bands = lax.axis_size("dom"), lax.axis_size("lat")
    rows, columns = states.shape[2:]
    blocks = columns // LANES
    wide = rows + 2 * HALO
    state_tiles, noise_tiles = row_tiles(states), row_tiles(stir_noise)
    table = jnp.swapaxes(ancestors, 1, 2)

    def pair(band, turn):
        partner = band + 1 if band % 2 == turn else band - 1
        return partner if 0 <= partner < bands else None

    def following(island, band):
        return (island + 1) % islands, band

    def beside(island, band):
        return (island ^ 1 if islands % 2 == 0 else (island + 1) % islands), band

    def across(turn, step):
        def place(island, band):
            partner = pair(band, turn)
            if partner is not None:
                return (island + step) % islands, partner
            return beside(island, band)

        return place

    def only(parity):
        def place(island, band):
            partner = pair(band, 1)
            if partner is None:
                return beside(island, band)
            if island % 2 == parity:
                return island, partner
            return (island + 2) % islands, band

        return place

    real = jnp.float32
    full, edge = (VMEM, (4 * rows, blocks, LANES), real), (VMEM, (3 * HALO + NEAR, blocks, LANES), real)
    later_rows = (VMEM, (states.shape[1] * rows, blocks, LANES), real)
    sends = {}
    sends["main"], state_tiles, noise_tiles, table = on_chip(
        functools.partial(collect, islands=islands),
        [HBM] * 3,
        [full, (VMEM, state_tiles.shape, real), (VMEM, noise_tiles.shape, real), (VMEM, table.shape, jnp.int32)],
        [pltpu.SemaphoreType.DMA((4,))],
    )(*(pltpu.with_memory_space_constraint(value, pltpu.HBM) for value in (state_tiles, noise_tiles, table)))
    sends["xa"], sends["xb"], sends["ka"], sends["kb"], kmain, later, plan = on_chip(
        functools.partial(edges, islands=islands),
        [VMEM] * 3,
        [edge] * 4 + [full, later_rows, (VMEM, (3, blocks, LANES), real)],
    )(state_tiles, noise_tiles, table)
    places = {
        "main": following,
        "xa": across(0, 1),
        "xb": across(1, 1),
        "ka": across(0, 0),
        "kb": only(1),
        "kc": only(0),
    }
    sends["kc"] = sends["kb"]
    got = {name: send(sends[name], places[name]) for name in ORDER}
    late_sources = (plan, got["main"], got["xa"], got["xb"], kmain, got["ka"], got["kb"], got["kc"], later)

    work = [pltpu.VMEM((3 * wide, blocks, LANES), real)] * 2 + [pltpu.VMEM((rows + 2 * NEAR, blocks, LANES), real)]
    result = (3,) + state_tiles.shape[2:]
    flops = 60 * wide * columns * 4 * STEPS
    sizes = dict(bands=bands)
    (inside,) = on_chip(
        functools.partial(inner, **sizes),
        [VMEM] * 5,
        [(VMEM, ((3 * HALO + 1) * rows, blocks, LANES), real)],
    )(plan, got["main"], kmain, got["xa"], got["xb"])
    (first,) = on_chip(
        functools.partial(outer, **sizes),
        [VMEM] * 7,
        [(VMEM, result, real)],
        [pltpu.VMEM((6 * HALO * HALO, blocks, LANES), real), pltpu.VMEM((2 * NEAR, blocks, LANES), real)],
    )(plan, inside, got["xa"], got["xb"], got["ka"], got["kb"], later)
    far = send(first, following)
    (second,) = on_chip(functools.partial(payload_even, **sizes), [VMEM] * 9, [(VMEM, result, real)], work, flops)(*late_sources)
    near = send(second, beside)
    (third,) = on_chip(functools.partial(keep_local, bands=bands), [VMEM] * 9, [(VMEM, result, real)], work, flops)(
        *late_sources
    )
    (out,) = on_chip(
        finish, [VMEM] * 5, [(HBM, state_tiles.shape, real)], [pltpu.SemaphoreType.DMA((2,))]
    )(plan, far, second, near, third)
    return from_row_tiles(out)


def solution(mesh):
    in_specs = (P(None, "dom", "lat", None), P(None, "dom", "lat", None), P())
    out_specs = P(None, "dom", "lat", None)
    return jax.shard_map(body, mesh=mesh, in_specs=in_specs, out_specs=out_specs, check_vma=False)
```
